256 devices in a mesh: seq: 32 (over x, y, core), head: 8 (over z).
Axes of the slice: x: 4, y: 4, z: 8, core: 2. Of those that a mesh axis runs over, the one named last changes fastest.
Arguments:
- queries: bfloat16 [32768, 4096], P(('seq', 'head')), may hold values from -40 to 40
- keys: bfloat16 [32768, 4096], P(('seq', 'head')), may hold values from -4 to 4
- values: bfloat16 [32768, 4096], P(('seq', 'head')), may hold values from -40 to 40
- grad_out: bfloat16 [32768, 4096], P(('seq', 'head')), may hold values from -40 to 40
Outputs:
- output: bfloat16 [32768, 4096], P(('seq', 'head'))
- grad_queries: bfloat16 [32768, 4096], P(('seq', 'head'))
- grad_keys: bfloat16 [32768, 4096], P(('seq', 'head'))
- grad_values: bfloat16 [32768, 4096], P(('seq', 'head'))
The draws below stay inside these ranges and needn't reach their ends.
All inputs are finite; a program needn't handle non-finite values.
Results may differ from the reference program's by a relative error of at most 0.01.
Values may be sent and summed in bfloat16 or wider, within the bound.
A program may use at most 128 MiB of HBM per device.

```python
import math
import jax
import jax.numpy as jnp
from jax import lax

HEADS = 32
DH = 128
L = 1024
D = 4096
TOKENS = 32768
N_SEQ = 32


def draw_queries(key, part):
    first, second = jax.random.split(jax.random.fold_in(key, 11))
    base = jnp.clip(jax.random.normal(first, (TOKENS, D), jnp.float32), -4.0, 4.0)
    scale = jnp.exp(jax.random.uniform(second, (TOKENS, 1), jnp.float32) * math.log(10.0))
    return (base * scale).astype(jnp.bfloat16)


def draw_values(key, part):
    first, second = jax.random.split(jax.random.fold_in(key, 23))
    base = jnp.clip(jax.random.normal(first, (TOKENS, D), jnp.float32), -4.0, 4.0)
    scale = jnp.exp(jax.random.uniform(second, (1, D), jnp.float32) * math.log(10.0))
    return (base * scale).astype(jnp.bfloat16)


def shard_levels(own_key, extent, cuts, least, top_value):
    loudness = 1.0
    for dim, shards_of in cuts:
        draws = jax.random.uniform(jax.random.fold_in(jax.random.fold_in(own_key, 6), dim), (shards_of,), jnp.float32, least / len(cuts), top_value / len(cuts))
        loudness = loudness * jnp.repeat(jnp.exp(draws), extent[dim] // shards_of).reshape((-1,) + (1,) * (len(extent) - 1 - dim))
    return loudness


def gaussian(own_key, dims, deviation, limit, shards=(), dtype=jnp.bfloat16):
    drawn = jax.random.normal(own_key, dims, jnp.float32) * deviation
    if len(shards) > 0:
        drawn = shard_levels(own_key, dims, shards, -0.22, 0.18) * drawn
    return jnp.clip(drawn, min=-limit, max=limit).astype(dtype)


def setup_inputs(seed: int = 0) -> dict:
    key_list = jax.random.split(jax.random.key(seed), 5)
    return {
        "queries": draw_queries(jax.random.fold_in(key_list[4], 71), 0),
        "keys": gaussian(key_list[1], (TOKENS, D), 1.0, 4.0, ((0, 256),)),
        "values": draw_values(jax.random.fold_in(key_list[4], 71), 0),
        "grad_out": gaussian(key_list[3], (TOKENS, D), 8.0, 40.0, ((0, 256),)),
    }


epsilon = 1e-06

def rounded(x):
    half = lax.optimization_barrier(x.astype(jnp.bfloat16))
    return half.astype(jnp.float32)

def feature_map(x):
    xf = x.astype(jnp.float32)
    return jnp.where(xf > 0, xf + 1.0, jnp.exp(jnp.minimum(xf, 0.0)))

def feature_slope(x):
    xf = x.astype(jnp.float32)
    return jnp.where(xf > 0, 1.0, jnp.exp(jnp.minimum(xf, 0.0)))

def block_core(query_blk, key_blk, value_blk, grad_blk, prefix_state):
    causal = jnp.arange(L)[:, None] >= jnp.arange(L)[None, :]
    query_feat = rounded(feature_map(query_blk))
    key_feat = rounded(feature_map(key_blk))
    value_f = value_blk.astype(jnp.float32)
    scores = jnp.einsum('thd,shd->hts', query_feat, key_feat)
    scores = rounded(jnp.where(causal[None], scores, 0.0))
    prefix_bf = rounded(prefix_state)
    mixed = jnp.einsum('hts,she->the', scores, value_f) + jnp.einsum('thd,hde->the', query_feat, prefix_bf)
    inv_rms = lax.rsqrt(lax.optimization_barrier(jnp.mean(mixed * mixed, -1, keepdims=True)) + epsilon)
    normed = mixed * inv_rms
    grad_norm = grad_blk.astype(jnp.float32)
    grad_mix = inv_rms * (grad_norm - normed * lax.optimization_barrier(jnp.mean(grad_norm * normed, -1, keepdims=True)))
    grad_mix = rounded(grad_mix)
    return (query_feat, key_feat, value_f, scores, prefix_bf, normed, grad_mix, causal)

def reference(queries, keys, values, grad_out):
    shape4 = (N_SEQ, L, HEADS, DH)
    query_blocks = queries.reshape(shape4)
    key_blocks = keys.reshape(shape4)
    value_blocks = values.reshape(shape4)
    grad_blocks = grad_out.reshape(shape4)

    def own_state(pair):
        key_feat = rounded(feature_map(pair[0]))
        return jnp.einsum('shd,she->hde', key_feat, pair[1].astype(jnp.float32))
    owns = lax.map(own_state, (key_blocks, value_blocks))
    running = jnp.cumsum(owns, 0)
    prefixes = jnp.concatenate([jnp.zeros_like(owns[:1]), running[:-1]], 0)

    def first_pass(items):
        core = block_core(*items)
        query_state = jnp.einsum('thd,the->hde', core[0], core[6])
        return (core[5].astype(jnp.bfloat16), query_state)
    normed_blocks, query_states = lax.map(first_pass, (query_blocks, key_blocks, value_blocks, grad_blocks, prefixes))
    backward_sum = jnp.cumsum(query_states[::-1], 0)[::-1]
    suffixes = jnp.concatenate([backward_sum[1:], jnp.zeros_like(query_states[:1])], 0)

    def second_pass(items):
        query_feat, key_feat, value_f, scores, prefix_bf, normed, grad_mix, causal = block_core(*items[:5])
        suffix_bf = rounded(items[5])
        grad_scores = jnp.einsum('the,she->hts', grad_mix, value_f)
        grad_scores = rounded(jnp.where(causal[None], grad_scores, 0.0))
        grad_qf = jnp.einsum('the,hde->thd', grad_mix, prefix_bf) + jnp.einsum('hts,shd->thd', grad_scores, key_feat)
        grad_kf = jnp.einsum('she,hde->shd', value_f, suffix_bf) + jnp.einsum('hts,thd->shd', grad_scores, query_feat)
        grad_vf = jnp.einsum('shd,hde->she', key_feat, suffix_bf) + jnp.einsum('hts,the->she', scores, grad_mix)
        grad_q = (grad_qf * feature_slope(items[0])).astype(jnp.bfloat16)
        grad_k = (grad_kf * feature_slope(items[1])).astype(jnp.bfloat16)
        return (grad_q, grad_k, grad_vf.astype(jnp.bfloat16))
    grad_q, grad_k, grad_v = lax.map(second_pass, (query_blocks, key_blocks, value_blocks, grad_blocks, prefixes, suffixes))
    flat = (TOKENS, D)
    return (normed_blocks.reshape(flat), grad_q.reshape(flat), grad_k.reshape(flat), grad_v.reshape(flat))
```

```python
import functools

import jax
import jax.numpy as jnp
from jax import lax
from jax.experimental import pallas as pl
from jax.experimental.pallas import tpu as pltpu
from jax.sharding import PartitionSpec as P

MESH = pl.DeviceIdType.MESH
DH = 128
HALF = DH // 2
UNROLL = 2
EPS = 1e-06
F32 = jnp.float32
BF16 = jnp.bfloat16


def dot_nn(a, b):
    return lax.dot_general(a, b, (((1,), (0,)), ((), ())), preferred_element_type=F32)


def dot_nt(a, b):
    return lax.dot_general(a, b, (((1,), (1,)), ((), ())), preferred_element_type=F32)


def dot_tn(a, b):
    return lax.dot_general(a, b, (((0,), (0,)), ((), ())), preferred_element_type=F32)


def feature_map(x):
    xf = x.astype(F32)
    return jnp.where(xf > 0, xf + 1.0, jnp.exp(jnp.minimum(xf, 0.0)))


def feature_slope(x):
    xf = x.astype(F32)
    return jnp.where(xf > 0, 1.0, jnp.exp(jnp.minimum(xf, 0.0)))


def kernel(
    groups, nz, npos,
    q_hbm, k_hbm, v_hbm, g_hbm,
    out_ref, gq_ref, gk_ref, gv_ref,
    q_in, k_in, v_in, g_in, q_feat, k_feat, gy_buf, mix_buf, pk_buf, pv_buf,
    load_sem, scan_a, scan_b,
):
    seq = lax.axis_index("seq")
    z = lax.axis_index("head")
    core = lax.rem(seq, 2)
    pos = lax.div(seq, 2)
    sibling = (seq + 1 - 2 * core, z)

    def z_peer(d):
        return lax.rem(z + d, nz)

    barrier = pltpu.get_barrier_semaphore()
    pl.semaphore_signal(barrier, inc=1, device_id=sibling, device_id_type=MESH)

    def greet_z(d, _):
        pl.semaphore_signal(barrier, inc=1, device_id=(seq, z_peer(d)), device_id_type=MESH)
        return 0

    def greet_pos(d, _):
        other = lax.rem(pos + d, npos) * 2 + core
        pl.semaphore_signal(barrier, inc=1, device_id=(other, z), device_id_type=MESH)
        return 0

    lax.fori_loop(1, nz, greet_z, 0)
    lax.fori_loop(1, npos, greet_pos, 0)

    def loads(k):
        cols = pl.ds(pl.multiple_of(k * (nz * DH), nz * DH), nz * DH)
        pairs = ((k_hbm, k_in), (v_hbm, v_in), (q_hbm, q_in), (g_hbm, g_in))
        return [
            pltpu.make_async_copy(src.at[:, cols], dst.at[:, cols], load_sem.at[i, k])
            for i, (src, dst) in enumerate(pairs)
        ]

    def start_loads(k, _):
        for copy in loads(k):
            copy.start()
        return 0

    lax.fori_loop(0, groups, start_loads, 0)

    row = lax.broadcasted_iota(jnp.int32, (DH, DH), 0)
    col = lax.broadcasted_iota(jnp.int32, (DH, DH), 1)
    lower = row >= col
    upper = col >= row

    def each_head(k, body):
        def step(i, _):
            for u in range(UNROLL):
                o = i * UNROLL + u
                body(o, pl.ds(pl.multiple_of((k * nz + o) * DH, DH), DH))
            return 0

        lax.fori_loop(0, nz // UNROLL, step, 0)

    def spread(bufs, name_src, name_dst, name_send, name_recv, k):
        src, dst = bufs[name_src], bufs[name_dst]

        def one(d, _):
            peer = z_peer(d)
            pltpu.make_async_remote_copy(
                src_ref=src.at[k, peer], dst_ref=dst.at[k, z],
                send_sem=bufs[name_send].at[k], recv_sem=bufs[name_recv].at[k],
                device_id=(seq, peer), device_id_type=MESH,
            ).start()
            return 0

        lax.fori_loop(1, nz, one, 0)
        dst[k, z] = src[k, z]

    def spread_desc(bufs, name_src, name_dst, name_send, name_recv, k):
        return pltpu.make_async_remote_copy(
            src_ref=bufs[name_src].at[k, pl.ds(0, nz - 1)],
            dst_ref=bufs[name_dst].at[k, pl.ds(0, nz - 1)],
            send_sem=bufs[name_send].at[k], recv_sem=bufs[name_recv].at[k],
            device_id=(seq, z_peer(1)), device_id_type=MESH,
        )

    IN = ("own", "held", "s_in", "r_in")
    BACK = ("ready", "carried", "s_back", "r_back")

    def sib_total(bufs, k):
        return pltpu.make_async_remote_copy(
            src_ref=bufs["total"].at[k, 1 - core], dst_ref=bufs["sib"].at[k],
            send_sem=bufs["s_sib"].at[0, k], recv_sem=bufs["r_sib"].at[0, k],
            device_id=sibling, device_id_type=MESH,
        )

    def sib_before(bufs, k):
        return pltpu.make_async_remote_copy(
            src_ref=bufs["half"].at[k], dst_ref=bufs["before"].at[k, core],
            send_sem=bufs["s_sib"].at[1, k], recv_sem=bufs["r_sib"].at[1, k],
            device_id=sibling, device_id_type=MESH,
        )

    def pos_copy(bufs, k, slot, other):
        return pltpu.make_async_remote_copy(
            src_ref=bufs["chip"].at[k], dst_ref=bufs["chips"].at[k, slot],
            send_sem=bufs["s_pos"].at[k, other], recv_sem=bufs["r_pos"].at[k, slot],
            device_id=(other * 2 + core, z), device_id_type=MESH,
        )

    def targets(forward):
        return (pos + 1, npos) if forward else (0, pos)

    def sources(forward):
        return (0, pos) if forward else (pos + 1, npos)

    def total_stage(bufs, forward, k):
        spread_desc(bufs, *IN, k).wait_recv()
        held = bufs["held"]
        total = held[k, 0].astype(F32)
        for i in range(1, nz):
            total = total + held[k, i].astype(F32)
        bufs["total"][k, 0] = total[:HALF]
        bufs["total"][k, 1] = total[HALF:]
        sib_total(bufs, k).start()

    def chip_stage(bufs, forward, k):
        sib_total(bufs, k).wait_recv()
        bufs["chip"][k] = (bufs["total"][k, core] + bufs["sib"][k]).astype(BF16)

        def one(other, _):
            pos_copy(bufs, k, pos, other).start()
            return 0

        lax.fori_loop(*targets(forward), one, 0)

    def before_stage(bufs, forward, k):
        def one(src, acc):
            pos_copy(bufs, k, src, src).wait_recv()
            return acc + bufs["chips"][k, src].astype(F32)

        earlier = lax.fori_loop(*sources(forward), one, jnp.zeros((HALF, DH), F32))
        first = core == (0 if forward else 1)
        bufs["before"][k, core] = jnp.where(first, earlier, earlier + bufs["sib"][k])
        bufs["half"][k] = jnp.where(first, earlier + bufs["total"][k, core], earlier)
        sib_before(bufs, k).start()

    def carry_stage(bufs, forward, k):
        sib_before(bufs, k).wait_recv()
        before = bufs["before"]
        run = jnp.concatenate([before[k, 0], before[k, 1]], axis=0)
        order = range(nz) if forward else range(nz - 1, -1, -1)
        for i in order:
            bufs["ready"][k, i] = run.astype(BF16)
            run = run + bufs["held"][k, i].astype(F32)
        spread(bufs, *BACK, k)

    def drain(bufs, forward):
        def one(k, _):
            spread_desc(bufs, *IN, k).wait_send()
            spread_desc(bufs, *BACK, k).wait_send()
            sib_total(bufs, k).wait_send()
            sib_before(bufs, k).wait_send()

            def sent(other, _):
                pos_copy(bufs, k, pos, other).wait_send()
                return 0

            lax.fori_loop(*targets(forward), sent, 0)
            return 0

        lax.fori_loop(0, groups, one, 0)

    def keys_compute(k):
        for copy in loads(k):
            copy.wait()

        def body(o, ds):
            kf = feature_map(k_in[:, ds]).astype(BF16)
            k_feat[:, ds] = kf
            scan_a["own"][k, o] = dot_tn(kf, v_in[:, ds]).astype(BF16)

        each_head(k, body)

    def inner_stage(k):
        def body(o, ds):
            qf = feature_map(q_in[:, ds]).astype(BF16)
            q_feat[:, ds] = qf
            scores = jnp.where(lower, dot_nt(qf, k_feat[:, ds]), 0.0).astype(BF16)
            mix_buf[:, ds] = dot_nn(scores, v_in[:, ds])

        each_head(k, body)

    def forward_stage(k):
        spread_desc(scan_a, *BACK, k).wait_recv()

        def body(o, ds):
            qf = q_feat[:, ds]
            mixed = mix_buf[:, ds] + dot_nn(qf, scan_a["carried"][k, o])
            inv = lax.rsqrt(jnp.mean(mixed * mixed, -1, keepdims=True) + EPS)
            normed = mixed * inv
            out_ref[:, ds] = normed.astype(BF16)
            grad = g_in[:, ds].astype(F32)
            gy = inv * (grad - normed * jnp.mean(grad * normed, -1, keepdims=True))
            gy = gy.astype(BF16)
            gy_buf[:, ds] = gy
            scan_b["own"][k, o] = dot_tn(qf, gy).astype(BF16)

        each_head(k, body)
        spread(scan_b, *IN, k)

    def query_stage(k):
        def body(o, ds):
            qf, kf, gy, v = q_feat[:, ds], k_feat[:, ds], gy_buf[:, ds], v_in[:, ds]
            m = jnp.where(lower, dot_nt(gy, v), 0.0).astype(BF16)
            dq = dot_nt(gy, scan_a["carried"][k, o]) + dot_nn(m, kf)
            gq_ref[:, ds] = (dq * feature_slope(q_in[:, ds])).astype(BF16)
            mt = jnp.where(upper, dot_nt(v, gy), 0.0).astype(BF16)
            pk_buf[:, ds] = dot_nn(mt, qf)
            at = jnp.where(upper, dot_nt(kf, qf), 0.0).astype(BF16)
            pv_buf[:, ds] = dot_nn(at, gy)

        each_head(k, body)

    def final_stage(k):
        spread_desc(scan_b, *BACK, k).wait_recv()

        def body(o, ds):
            u = scan_b["carried"][k, o]
            dk = dot_nt(v_in[:, ds], u) + pk_buf[:, ds]
            gk_ref[:, ds] = (dk * feature_slope(k_in[:, ds])).astype(BF16)
            gv_ref[:, ds] = (dot_nn(k_feat[:, ds], u) + pv_buf[:, ds]).astype(BF16)

        each_head(k, body)

    keys_compute(0)
    pl.semaphore_wait(barrier, nz + npos - 1)
    spread(scan_a, *IN, 0)

    def start_group(k, _):
        keys_compute(k)
        spread(scan_a, *IN, k)
        return 0

    lax.fori_loop(1, groups, start_group, 0)

    a0 = 0
    f0 = groups
    b0 = 2 * groups - 1
    e0 = 3 * groups - 1
    plan = [
        (a0, functools.partial(total_stage, scan_a, True)),
        (a0 + 1, functools.partial(before_stage, scan_a, True)),
        (a0, inner_stage),
        (a0, functools.partial(chip_stage, scan_a, True)),
        (f0, forward_stage),
        (a0 + 1, functools.partial(carry_stage, scan_a, True)),
        (b0, functools.partial(total_stage, scan_b, False)),
        (b0 + 1, functools.partial(before_stage, scan_b, False)),
        (b0, query_stage),
        (b0, functools.partial(chip_stage, scan_b, False)),
        (b0 + 1, functools.partial(carry_stage, scan_b, False)),
        (e0, final_stage),
    ]

    def tick(t, _):
        for at, stage in plan:
            @pl.when((t >= at) & (t < at + groups))
            def _():
                stage(t - at)

        return 0

    lax.fori_loop(0, e0 + groups, tick, 0)
    drain(scan_a, True)
    drain(scan_b, False)


def scan_buffers(groups, nz, npos):
    dma = pltpu.SemaphoreType.DMA
    states = pltpu.VMEM((groups, nz, DH, DH), BF16)
    halves = pltpu.VMEM((groups, HALF, DH), F32)
    wholes = pltpu.VMEM((groups, 2, HALF, DH), F32)
    return {
        "own": states, "held": states, "ready": states, "carried": states,
        "total": wholes, "before": wholes, "sib": halves, "half": halves,
        "chip": pltpu.VMEM((groups, HALF, DH), BF16),
        "chips": pltpu.VMEM((groups, npos, HALF, DH), BF16),
        "s_in": dma((groups,)), "r_in": dma((groups,)),
        "s_back": dma((groups,)), "r_back": dma((groups,)),
        "s_sib": dma((2, groups)), "r_sib": dma((2, groups)),
        "s_pos": dma((groups, npos)), "r_pos": dma((groups, npos)),
    }


def solution(mesh):
    nz = mesh.shape["head"]
    npos = mesh.shape["seq"] // 2
    placed = P(("seq", "head"), None)

    def local(queries, keys, values, grad_out):
        rows, width = queries.shape
        groups = width // DH // nz
        half = pltpu.VMEM((rows, width), BF16)
        full = pltpu.VMEM((rows, width), F32)
        return pl.pallas_call(
            functools.partial(kernel, groups, nz, npos),
            out_shape=[jax.ShapeDtypeStruct((rows, width), BF16)] * 4,
            in_specs=[pl.BlockSpec(memory_space=pl.ANY)] * 4,
            out_specs=[pl.BlockSpec(memory_space=pltpu.VMEM)] * 4,
            scratch_shapes=[half] * 7 + [full] * 3 + [
                pltpu.SemaphoreType.DMA((4, groups)),
                scan_buffers(groups, nz, npos),
                scan_buffers(groups, nz, npos),
            ],
            compiler_params=pltpu.CompilerParams(
                collective_id=0, has_side_effects=True, vmem_limit_bytes=44 * 2**20
            ),
        )(queries, keys, values, grad_out)

    return jax.shard_map(
        local, mesh=mesh, in_specs=(placed,) * 4, out_specs=(placed,) * 4, check_vma=False
    )
```

```python
import functools

import jax
import jax.numpy as jnp
from jax import lax
from jax.experimental import pallas as pl
from jax.experimental.pallas import tpu as pltpu
from jax.sharding import PartitionSpec as P

MESH = pl.DeviceIdType.MESH
DH = 128
HALF = DH // 2
UNROLL = 4
EPS = 1e-06
F32 = jnp.float32
BF16 = jnp.bfloat16

PLAN = (
    ("total_a", (0, 1, 2, 3)),
    ("before_a", (2, 3, 4, 5)),
    ("chip_a", (0, 1, 2, 3)),
    ("total_b", (7, 9, 10, 11)),
    ("carry_a", (2, 3, 4, 6)),
    ("carry_b", (10, 11, 12, 13)),
    ("inner", (3, 4, 5, 7)),
    ("forward", (4, 6, 7, 8)),
    ("chip_b", (7, 9, 10, 11)),
    ("query", (5, 6, 7, 12)),
    ("before_b", (9, 10, 11, 12)),
    ("final", (11, 13, 14, 15)),
)


def dot_nn(a, b):
    return lax.dot_general(a, b, (((1,), (0,)), ((), ())), preferred_element_type=F32)


def dot_nt(a, b):
    return lax.dot_general(a, b, (((1,), (1,)), ((), ())), preferred_element_type=F32)


def dot_tn(a, b):
    return lax.dot_general(a, b, (((0,), (0,)), ((), ())), preferred_element_type=F32)


def feature_map(x):
    xf = x.astype(F32)
    return jnp.where(xf > 0, xf + 1.0, jnp.exp(jnp.minimum(xf, 0.0)))


def feature_slope(x):
    xf = x.astype(F32)
    return jnp.where(xf > 0, 1.0, jnp.exp(jnp.minimum(xf, 0.0)))


def kernel(
    groups, nz, npos,
    q_hbm, k_hbm, v_hbm, g_hbm,
    out_ref, gq_ref, gk_ref, gv_ref,
    q_in, k_in, v_in, g_in, q_feat, k_feat, gy_buf, mix_buf, pk_buf, pv_buf,
    load_sem, scan_a, scan_b,
):
    seq = lax.axis_index("seq")
    z = lax.axis_index("head")
    core = lax.rem(seq, 2)
    pos = lax.div(seq, 2)
    sibling = (seq + 1 - 2 * core, z)

    def z_peer(d):
        return lax.rem(z + d, nz)

    def loads(k, *chosen):
        cols = pl.ds(pl.multiple_of(k * (nz * DH), nz * DH), nz * DH)
        pairs = ((k_hbm, k_in), (v_hbm, v_in), (q_hbm, q_in), (g_hbm, g_in))
        return [
            pltpu.make_async_copy(src.at[:, cols], dst.at[:, cols], load_sem.at[i, k])
            for i, (src, dst) in enumerate(pairs)
            if i in chosen
        ]

    def start_loads(*chosen):
        def one(k, _):
            for copy in loads(k, *chosen):
                copy.start()
            return 0

        lax.fori_loop(0, groups, one, 0)

    start_loads(0, 1)
    start_loads(2, 3)

    barrier = pltpu.get_barrier_semaphore()
    pl.semaphore_signal(barrier, inc=1, device_id=sibling, device_id_type=MESH)

    def greet_z(d, _):
        pl.semaphore_signal(barrier, inc=1, device_id=(seq, z_peer(d)), device_id_type=MESH)
        return 0

    def greet_pos(d, _):
        other = lax.rem(pos + d, npos) * 2 + core
        pl.semaphore_signal(barrier, inc=1, device_id=(other, z), device_id_type=MESH)
        return 0

    lax.fori_loop(1, nz, greet_z, 0)
    lax.fori_loop(1, npos, greet_pos, 0)

    row = lax.broadcasted_iota(jnp.int32, (DH, DH), 0)
    col = lax.broadcasted_iota(jnp.int32, (DH, DH), 1)
    lower = row >= col
    upper = col >= row

    unroll = min(UNROLL, nz)

    def each_head(k, body):
        def step(i, _):
            for u in range(unroll):
                o = i * unroll + u
                body(o, pl.ds(pl.multiple_of((k * nz + o) * DH, DH), DH))
            return 0

        lax.fori_loop(0, nz // unroll, step, 0)

    def spread(bufs, name_src, name_dst, name_send, name_recv, k):
        src, dst = bufs[name_src], bufs[name_dst]

        def one(d, _):
            peer = z_peer(d)
            pltpu.make_async_remote_copy(
                src_ref=src.at[k, peer], dst_ref=dst.at[k, z],
                send_sem=bufs[name_send].at[k], recv_sem=bufs[name_recv].at[k],
                device_id=(seq, peer), device_id_type=MESH,
            ).start()
            return 0

        lax.fori_loop(1, nz, one, 0)
        dst[k, z] = src[k, z]

    def spread_desc(bufs, name_src, name_dst, name_send, name_recv, k):
        return pltpu.make_async_remote_copy(
            src_ref=bufs[name_src].at[k, pl.ds(0, nz - 1)],
            dst_ref=bufs[name_dst].at[k, pl.ds(0, nz - 1)],
            send_sem=bufs[name_send].at[k], recv_sem=bufs[name_recv].at[k],
            device_id=(seq, z_peer(1)), device_id_type=MESH,
        )

    IN = ("own", "held", "s_in", "r_in")
    BACK = ("ready", "carried", "s_back", "r_back")

    def sib_total(bufs, k):
        return pltpu.make_async_remote_copy(
            src_ref=bufs["total"].at[k, 1 - core], dst_ref=bufs["sib"].at[k],
            send_sem=bufs["s_sib"].at[0, k], recv_sem=bufs["r_sib"].at[0, k],
            device_id=sibling, device_id_type=MESH,
        )

    def sib_before(bufs, k):
        return pltpu.make_async_remote_copy(
            src_ref=bufs["half"].at[k], dst_ref=bufs["before"].at[k, core],
            send_sem=bufs["s_sib"].at[1, k], recv_sem=bufs["r_sib"].at[1, k],
            device_id=sibling, device_id_type=MESH,
        )

    def pos_copy(bufs, k, slot, other):
        return pltpu.make_async_remote_copy(
            src_ref=bufs["chip"].at[k], dst_ref=bufs["chips"].at[k, slot],
            send_sem=bufs["s_pos"].at[k, other], recv_sem=bufs["r_pos"].at[k, slot],
            device_id=(other * 2 + core, z), device_id_type=MESH,
        )

    def targets(forward):
        return (pos + 1, npos) if forward else (0, pos)

    def sources(forward):
        return (0, pos) if forward else (pos + 1, npos)

    def total_stage(bufs, forward, k):
        spread_desc(bufs, *IN, k).wait_recv()
        held = bufs["held"]
        total = held[k, 0].astype(F32)
        for i in range(1, nz):
            total = total + held[k, i].astype(F32)
        bufs["total"][k, 0] = total[:HALF]
        bufs["total"][k, 1] = total[HALF:]
        sib_total(bufs, k).start()

    def chip_stage(bufs, forward, k):
        sib_total(bufs, k).wait_recv()
        bufs["chip"][k] = (bufs["total"][k, core] + bufs["sib"][k]).astype(BF16)

        def one(other, _):
            pos_copy(bufs, k, pos, other).start()
            return 0

        lax.fori_loop(*targets(forward), one, 0)

    def before_stage(bufs, forward, k):
        def one(src, acc):
            pos_copy(bufs, k, src, src).wait_recv()
            return acc + bufs["chips"][k, src].astype(F32)

        earlier = lax.fori_loop(*sources(forward), one, jnp.zeros((HALF, DH), F32))
        first = core == (0 if forward else 1)
        bufs["before"][k, core] = jnp.where(first, earlier, earlier + bufs["sib"][k])
        bufs["half"][k] = jnp.where(first, earlier + bufs["total"][k, core], earlier)
        sib_before(bufs, k).start()

    def carry_stage(bufs, forward, k):
        sib_before(bufs, k).wait_recv()
        before = bufs["before"]
        run = jnp.concatenate([before[k, 0], before[k, 1]], axis=0)
        order = range(nz) if forward else range(nz - 1, -1, -1)
        for i in order:
            bufs["ready"][k, i] = run.astype(BF16)
            run = run + bufs["held"][k, i].astype(F32)
        spread(bufs, *BACK, k)

    def drain(bufs, forward):
        def one(k, _):
            spread_desc(bufs, *IN, k).wait_send()
            spread_desc(bufs, *BACK, k).wait_send()
            sib_total(bufs, k).wait_send()
            sib_before(bufs, k).wait_send()

            def sent(other, _):
                pos_copy(bufs, k, pos, other).wait_send()
                return 0

            lax.fori_loop(*targets(forward), sent, 0)
            return 0

        lax.fori_loop(0, groups, one, 0)

    def keys_compute(k):
        for copy in loads(k, 0, 1):
            copy.wait()

        def body(o, ds):
            kf = feature_map(k_in[:, ds]).astype(BF16)
            k_feat[:, ds] = kf
            scan_a["own"][k, o] = dot_tn(kf, v_in[:, ds]).astype(BF16)

        each_head(k, body)

    def inner_stage(k):
        loads(k, 2)[0].wait()

        def body(o, ds):
            qf = feature_map(q_in[:, ds]).astype(BF16)
            q_feat[:, ds] = qf
            scores = jnp.where(lower, dot_nt(qf, k_feat[:, ds]), 0.0).astype(BF16)
            mix_buf[:, ds] = dot_nn(scores, v_in[:, ds])

        each_head(k, body)

    def forward_stage(k):
        loads(k, 3)[0].wait()
        spread_desc(scan_a, *BACK, k).wait_recv()

        def body(o, ds):
            qf = q_feat[:, ds]
            mixed = mix_buf[:, ds] + dot_nn(qf, scan_a["carried"][k, o])
            inv = lax.rsqrt(jnp.mean(mixed * mixed, -1, keepdims=True) + EPS)
            normed = mixed * inv
            out_ref[:, ds] = normed.astype(BF16)
            grad = g_in[:, ds].astype(F32)
            gy = inv * (grad - normed * jnp.mean(grad * normed, -1, keepdims=True))
            gy = gy.astype(BF16)
            gy_buf[:, ds] = gy
            scan_b["own"][k, o] = dot_tn(qf, gy).astype(BF16)

        each_head(k, body)
        spread(scan_b, *IN, k)

    def query_stage(k):
        def body(o, ds):
            qf, kf, gy, v = q_feat[:, ds], k_feat[:, ds], gy_buf[:, ds], v_in[:, ds]
            m = jnp.where(lower, dot_nt(gy, v), 0.0).astype(BF16)
            dq = dot_nt(gy, scan_a["carried"][k, o]) + dot_nn(m, kf)
            gq_ref[:, ds] = (dq * feature_slope(q_in[:, ds])).astype(BF16)
            mt = jnp.where(upper, dot_nt(v, gy), 0.0).astype(BF16)
            pk_buf[:, ds] = dot_nn(mt, qf)
            at = jnp.where(upper, dot_nt(kf, qf), 0.0).astype(BF16)
            pv_buf[:, ds] = dot_nn(at, gy)

        each_head(k, body)

    def final_stage(k):
        spread_desc(scan_b, *BACK, k).wait_recv()

        def body(o, ds):
            u = scan_b["carried"][k, o]
            dk = dot_nt(v_in[:, ds], u) + pk_buf[:, ds]
            gk_ref[:, ds] = (dk * feature_slope(k_in[:, ds])).astype(BF16)
            gv_ref[:, ds] = (dot_nn(k_feat[:, ds], u) + pv_buf[:, ds]).astype(BF16)

        each_head(k, body)

    keys_compute(0)
    pl.semaphore_wait(barrier, nz + npos - 1)
    spread(scan_a, *IN, 0)

    def start_group(k, _):
        keys_compute(k)
        spread(scan_a, *IN, k)
        return 0

    lax.fori_loop(1, groups, start_group, 0)

    stages = {
        "total_a": functools.partial(total_stage, scan_a, True),
        "chip_a": functools.partial(chip_stage, scan_a, True),
        "before_a": functools.partial(before_stage, scan_a, True),
        "carry_a": functools.partial(carry_stage, scan_a, True),
        "total_b": functools.partial(total_stage, scan_b, False),
        "chip_b": functools.partial(chip_stage, scan_b, False),
        "before_b": functools.partial(before_stage, scan_b, False),
        "carry_b": functools.partial(carry_stage, scan_b, False),
        "inner": inner_stage,
        "forward": forward_stage,
        "query": query_stage,
        "final": final_stage,
    }

    def tick(t, _):
        for name, at in PLAN:
            here = functools.reduce(jnp.logical_or, [t == a for a in at])

            @pl.when(here)
            def _():
                with jax.named_scope(name):
                    stages[name](sum((t >= a).astype(jnp.int32) for a in at[1:]))

        return 0

    lax.fori_loop(0, 1 + max(max(at) for _, at in PLAN), tick, 0)
    drain(scan_a, True)
    drain(scan_b, False)


def scan_buffers(groups, nz, npos):
    dma = pltpu.SemaphoreType.DMA
    states = pltpu.VMEM((groups, nz, DH, DH), BF16)
    halves = pltpu.VMEM((groups, HALF, DH), F32)
    wholes = pltpu.VMEM((groups, 2, HALF, DH), F32)
    return {
        "own": states, "held": states, "ready": states, "carried": states,
        "total": wholes, "before": wholes, "sib": halves, "half": halves,
        "chip": pltpu.VMEM((groups, HALF, DH), BF16),
        "chips": pltpu.VMEM((groups, npos, HALF, DH), BF16),
        "s_in": dma((groups,)), "r_in": dma((groups,)),
        "s_back": dma((groups,)), "r_back": dma((groups,)),
        "s_sib": dma((2, groups)), "r_sib": dma((2, groups)),
        "s_pos": dma((groups, npos)), "r_pos": dma((groups, npos)),
    }


def solution(mesh):
    nz = mesh.shape["head"]
    npos = mesh.shape["seq"] // 2
    placed = P(("seq", "head"), None)

    def local(queries, keys, values, grad_out):
        rows, width = queries.shape
        groups = width // DH // nz
        half = pltpu.VMEM((rows, width), BF16)
        full = pltpu.VMEM((rows, width), F32)
        return pl.pallas_call(
            functools.partial(kernel, groups, nz, npos),
            out_shape=[jax.ShapeDtypeStruct((rows, width), BF16)] * 4,
            in_specs=[pl.BlockSpec(memory_space=pltpu.HBM)] * 4,
            out_specs=[pl.BlockSpec(memory_space=pltpu.VMEM)] * 4,
            scratch_shapes=[half] * 7 + [full] * 3 + [
                pltpu.SemaphoreType.DMA((4, groups)),
                scan_buffers(groups, nz, npos),
                scan_buffers(groups, nz, npos),
            ],
            compiler_params=pltpu.CompilerParams(
                collective_id=0, has_side_effects=True, vmem_limit_bytes=49 * 2**20
            ),
        )(queries, keys, values, grad_out)

    return jax.shard_map(
        local, mesh=mesh, in_specs=(placed,) * 4, out_specs=(placed,) * 4, check_vma=False
    )
```

```python
import functools

import jax
import jax.numpy as jnp
from jax import lax
from jax.experimental import pallas as pl
from jax.experimental.pallas import tpu as pltpu
from jax.sharding import PartitionSpec as P

MESH = pl.DeviceIdType.MESH
DH = 128
HALF = DH // 2
UNROLL = 8
EPS = 1e-06
F32 = jnp.float32
BF16 = jnp.bfloat16

PLAN = (
    ("total_a", (0, 1, 2, 3)),
    ("before_a", (2, 3, 4, 5)),
    ("chip_a", (0, 1, 2, 3)),
    ("total_b", (7, 9, 10, 11)),
    ("carry_a", (2, 3, 4, 6)),
    ("carry_b", (10, 11, 12, 13)),
    ("inner", (3, 4, 5, 7)),
    ("forward", (4, 6, 7, 8)),
    ("chip_b", (7, 9, 10, 11)),
    ("query", (5, 6, 7, 12)),
    ("before_b", (9, 10, 11, 12)),
    ("final", (11, 13, 14, 15)),
)


def dot_nn(a, b):
    return lax.dot_general(a, b, (((1,), (0,)), ((), ())), preferred_element_type=F32)


def dot_nt(a, b):
    return lax.dot_general(a, b, (((1,), (1,)), ((), ())), preferred_element_type=F32)


def dot_tn(a, b):
    return lax.dot_general(a, b, (((0,), (0,)), ((), ())), preferred_element_type=F32)


def feature_map(x):
    xf = x.astype(F32)
    return jnp.where(xf > 0, xf + 1.0, jnp.exp(jnp.minimum(xf, 0.0)))


def feature_slope(x):
    xf = x.astype(F32)
    return jnp.where(xf > 0, 1.0, jnp.exp(jnp.minimum(xf, 0.0)))


def kernel(
    groups, nz, npos,
    q_hbm, k_hbm, v_hbm, g_hbm,
    out_ref, gq_ref, gk_ref, gv_ref,
    q_in, k_in, v_in, g_in, q_feat, k_feat, gy_buf, mix_buf, pk_buf, pv_buf,
    load_sem, scan_a, scan_b,
):
    seq = lax.axis_index("seq")
    z = lax.axis_index("head")
    core = lax.rem(seq, 2)
    pos = lax.div(seq, 2)
    sibling = (seq + 1 - 2 * core, z)

    def z_peer(d):
        return lax.rem(z + d, nz)

    def loads(k, *chosen):
        cols = pl.ds(pl.multiple_of(k * (nz * DH), nz * DH), nz * DH)
        pairs = ((k_hbm, k_in), (v_hbm, v_in), (q_hbm, q_in), (g_hbm, g_in))
        return [
            pltpu.make_async_copy(src.at[:, cols], dst.at[:, cols], load_sem.at[i, k])
            for i, (src, dst) in enumerate(pairs)
            if i in chosen
        ]

    def start_loads(*chosen):
        def one(k, _):
            for copy in loads(k, *chosen):
                copy.start()
            return 0

        lax.fori_loop(0, groups, one, 0)

    start_loads(0, 1)
    start_loads(2, 3)

    barrier = pltpu.get_barrier_semaphore()
    pl.semaphore_signal(barrier, inc=1, device_id=sibling, device_id_type=MESH)

    def greet_z(d, _):
        pl.semaphore_signal(barrier, inc=1, device_id=(seq, z_peer(d)), device_id_type=MESH)
        return 0

    def greet_pos(d, _):
        other = lax.rem(pos + d, npos) * 2 + core
        pl.semaphore_signal(barrier, inc=1, device_id=(other, z), device_id_type=MESH)
        return 0

    lax.fori_loop(1, nz, greet_z, 0)
    lax.fori_loop(1, npos, greet_pos, 0)

    row = lax.broadcasted_iota(jnp.int32, (DH, DH), 0)
    col = lax.broadcasted_iota(jnp.int32, (DH, DH), 1)
    lower = row >= col
    upper = col >= row

    unroll = min(UNROLL, nz)

    def each_head(k, body):
        def step(i, _):
            for u in range(unroll):
                o = i * unroll + u
                body(o, pl.ds(pl.multiple_of((k * nz + o) * DH, DH), DH))
            return 0

        lax.fori_loop(0, nz // unroll, step, 0)

    def spread(bufs, name_src, name_dst, name_send, name_recv, k):
        src, dst = bufs[name_src], bufs[name_dst]

        def one(d, _):
            peer = z_peer(d)
            pltpu.make_async_remote_copy(
                src_ref=src.at[k, peer], dst_ref=dst.at[k, z],
                send_sem=bufs[name_send].at[k], recv_sem=bufs[name_recv].at[k],
                device_id=(seq, peer), device_id_type=MESH,
            ).start()
            return 0

        lax.fori_loop(1, nz, one, 0)
        dst[k, z] = src[k, z]

    def spread_desc(bufs, name_src, name_dst, name_send, name_recv, k):
        return pltpu.make_async_remote_copy(
            src_ref=bufs[name_src].at[k, pl.ds(0, nz - 1)],
            dst_ref=bufs[name_dst].at[k, pl.ds(0, nz - 1)],
            send_sem=bufs[name_send].at[k], recv_sem=bufs[name_recv].at[k],
            device_id=(seq, z_peer(1)), device_id_type=MESH,
        )

    IN = ("own", "held", "s_in", "r_in")
    BACK = ("ready", "carried", "s_back", "r_back")

    def sib_total(bufs, k):
        return pltpu.make_async_remote_copy(
            src_ref=bufs["total"].at[k, 1 - core], dst_ref=bufs["sib"].at[k],
            send_sem=bufs["s_sib"].at[0, k], recv_sem=bufs["r_sib"].at[0, k],
            device_id=sibling, device_id_type=MESH,
        )

    def sib_before(bufs, k):
        return pltpu.make_async_remote_copy(
            src_ref=bufs["half"].at[k], dst_ref=bufs["before"].at[k, core],
            send_sem=bufs["s_sib"].at[1, k], recv_sem=bufs["r_sib"].at[1, k],
            device_id=sibling, device_id_type=MESH,
        )

    def pos_copy(bufs, k, slot, other):
        return pltpu.make_async_remote_copy(
            src_ref=bufs["chip"].at[k], dst_ref=bufs["chips"].at[k, slot],
            send_sem=bufs["s_pos"].at[k, other], recv_sem=bufs["r_pos"].at[k, slot],
            device_id=(other * 2 + core, z), device_id_type=MESH,
        )

    def targets(forward):
        return (pos + 1, npos) if forward else (0, pos)

    def sources(forward):
        return (0, pos) if forward else (pos + 1, npos)

    def total_stage(bufs, forward, k):
        spread_desc(bufs, *IN, k).wait_recv()
        held = bufs["held"]
        total = held[k, 0].astype(F32)
        for i in range(1, nz):
            total = total + held[k, i].astype(F32)
        bufs["total"][k, 0] = total[:HALF]
        bufs["total"][k, 1] = total[HALF:]
        sib_total(bufs, k).start()

    def chip_stage(bufs, forward, k):
        sib_total(bufs, k).wait_recv()
        bufs["chip"][k] = (bufs["total"][k, core] + bufs["sib"][k]).astype(BF16)

        def one(other, _):
            pos_copy(bufs, k, pos, other).start()
            return 0

        lax.fori_loop(*targets(forward), one, 0)

    def before_stage(bufs, forward, k):
        def one(src, acc):
            pos_copy(bufs, k, src, src).wait_recv()
            return acc + bufs["chips"][k, src].astype(F32)

        earlier = lax.fori_loop(*sources(forward), one, jnp.zeros((HALF, DH), F32))
        first = core == (0 if forward else 1)
        bufs["before"][k, core] = jnp.where(first, earlier, earlier + bufs["sib"][k])
        bufs["half"][k] = jnp.where(first, earlier + bufs["total"][k, core], earlier)
        sib_before(bufs, k).start()

    def carry_stage(bufs, forward, k):
        sib_before(bufs, k).wait_recv()
        before = bufs["before"]
        run = jnp.concatenate([before[k, 0], before[k, 1]], axis=0)
        order = range(nz) if forward else range(nz - 1, -1, -1)
        for i in order:
            bufs["ready"][k, i] = run.astype(BF16)
            run = run + bufs["held"][k, i].astype(F32)
        spread(bufs, *BACK, k)

    def drain(bufs, forward):
        def one(k, _):
            spread_desc(bufs, *IN, k).wait_send()
            spread_desc(bufs, *BACK, k).wait_send()
            sib_total(bufs, k).wait_send()
            sib_before(bufs, k).wait_send()

            def sent(other, _):
                pos_copy(bufs, k, pos, other).wait_send()
                return 0

            lax.fori_loop(*targets(forward), sent, 0)
            return 0

        lax.fori_loop(0, groups, one, 0)

    def keys_compute(k):
        for copy in loads(k, 0, 1):
            copy.wait()

        def body(o, ds):
            kf = feature_map(k_in[:, ds]).astype(BF16)
            k_feat[:, ds] = kf
            scan_a["own"][k, o] = dot_tn(kf, v_in[:, ds]).astype(BF16)

        each_head(k, body)

    def inner_stage(k):
        loads(k, 2)[0].wait()

        def body(o, ds):
            qf = feature_map(q_in[:, ds]).astype(BF16)
            q_feat[:, ds] = qf
            scores = jnp.where(lower, dot_nt(qf, k_feat[:, ds]), 0.0).astype(BF16)
            mix_buf[:, ds] = dot_nn(scores, v_in[:, ds])

        each_head(k, body)

    def forward_stage(k):
        loads(k, 3)[0].wait()
        spread_desc(scan_a, *BACK, k).wait_recv()

        def body(o, ds):
            qf = q_feat[:, ds]
            mixed = mix_buf[:, ds] + dot_nn(qf, scan_a["carried"][k, o])
            inv = lax.rsqrt(jnp.mean(mixed * mixed, -1, keepdims=True) + EPS)
            normed = mixed * inv
            out_ref[:, ds] = normed.astype(BF16)
            grad = g_in[:, ds].astype(F32)
            gy = inv * (grad - normed * jnp.mean(grad * normed, -1, keepdims=True))
            gy = gy.astype(BF16)
            gy_buf[:, ds] = gy
            scan_b["own"][k, o] = dot_tn(qf, gy).astype(BF16)

        each_head(k, body)
        spread(scan_b, *IN, k)

    def query_stage(k):
        def body(o, ds):
            qf, kf, gy, v = q_feat[:, ds], k_feat[:, ds], gy_buf[:, ds], v_in[:, ds]
            m = jnp.where(lower, dot_nt(gy, v), 0.0).astype(BF16)
            dq = dot_nt(gy, scan_a["carried"][k, o]) + dot_nn(m, kf)
            gq_ref[:, ds] = (dq * feature_slope(q_in[:, ds])).astype(BF16)
            mt = jnp.where(upper, dot_nt(v, gy), 0.0).astype(BF16)
            pk_buf[:, ds] = dot_nn(mt, qf)
            at = jnp.where(upper, dot_nt(kf, qf), 0.0).astype(BF16)
            pv_buf[:, ds] = dot_nn(at, gy)

        each_head(k, body)

    def final_stage(k):
        spread_desc(scan_b, *BACK, k).wait_recv()

        def body(o, ds):
            u = scan_b["carried"][k, o]
            dk = dot_nt(v_in[:, ds], u) + pk_buf[:, ds]
            gk_ref[:, ds] = (dk * feature_slope(k_in[:, ds])).astype(BF16)
            gv_ref[:, ds] = (dot_nn(k_feat[:, ds], u) + pv_buf[:, ds]).astype(BF16)

        each_head(k, body)

    keys_compute(0)
    pl.semaphore_wait(barrier, nz + npos - 1)
    spread(scan_a, *IN, 0)

    def start_group(k, _):
        keys_compute(k)
        spread(scan_a, *IN, k)
        return 0

    lax.fori_loop(1, groups, start_group, 0)

    stages = {
        "total_a": functools.partial(total_stage, scan_a, True),
        "chip_a": functools.partial(chip_stage, scan_a, True),
        "before_a": functools.partial(before_stage, scan_a, True),
        "carry_a": functools.partial(carry_stage, scan_a, True),
        "total_b": functools.partial(total_stage, scan_b, False),
        "chip_b": functools.partial(chip_stage, scan_b, False),
        "before_b": functools.partial(before_stage, scan_b, False),
        "carry_b": functools.partial(carry_stage, scan_b, False),
        "inner": inner_stage,
        "forward": forward_stage,
        "query": query_stage,
        "final": final_stage,
    }

    def tick(t, _):
        for name, at in PLAN:
            here = functools.reduce(jnp.logical_or, [t == a for a in at])

            @pl.when(here)
            def _():
                with jax.named_scope(name):
                    stages[name](sum((t >= a).astype(jnp.int32) for a in at[1:]))

        return 0

    lax.fori_loop(0, 1 + max(max(at) for _, at in PLAN), tick, 0)
    drain(scan_a, True)
    drain(scan_b, False)


def scan_buffers(groups, nz, npos):
    dma = pltpu.SemaphoreType.DMA
    states = pltpu.VMEM((groups, nz, DH, DH), BF16)
    halves = pltpu.VMEM((groups, HALF, DH), F32)
    wholes = pltpu.VMEM((groups, 2, HALF, DH), F32)
    return {
        "own": states, "held": states, "ready": states, "carried": states,
        "total": wholes, "before": wholes, "sib": halves, "half": halves,
        "chip": pltpu.VMEM((groups, HALF, DH), BF16),
        "chips": pltpu.VMEM((groups, npos, HALF, DH), BF16),
        "s_in": dma((groups,)), "r_in": dma((groups,)),
        "s_back": dma((groups,)), "r_back": dma((groups,)),
        "s_sib": dma((2, groups)), "r_sib": dma((2, groups)),
        "s_pos": dma((groups, npos)), "r_pos": dma((groups, npos)),
    }


def solution(mesh):
    nz = mesh.shape["head"]
    npos = mesh.shape["seq"] // 2
    placed = P(("seq", "head"), None)

    def local(queries, keys, values, grad_out):
        rows, width = queries.shape
        groups = width // DH // nz
        half = pltpu.VMEM((rows, width), BF16)
        full = pltpu.VMEM((rows, width), F32)
        return pl.pallas_call(
            functools.partial(kernel, groups, nz, npos),
            out_shape=[jax.ShapeDtypeStruct((rows, width), BF16)] * 4,
            in_specs=[pl.BlockSpec(memory_space=pltpu.HBM)] * 4,
            out_specs=[pl.BlockSpec(memory_space=pltpu.VMEM)] * 4,
            scratch_shapes=[half] * 7 + [full] * 3 + [
                pltpu.SemaphoreType.DMA((4, groups)),
                scan_buffers(groups, nz, npos),
                scan_buffers(groups, nz, npos),
            ],
            compiler_params=pltpu.CompilerParams(
                collective_id=0, has_side_effects=True, vmem_limit_bytes=49 * 2**20
            ),
        )(queries, keys, values, grad_out)

    return jax.shard_map(
        local, mesh=mesh, in_specs=(placed,) * 4, out_specs=(placed,) * 4, check_vma=False
    )
```

```python
import functools

import jax
import jax.numpy as jnp
from jax import lax
from jax.experimental import pallas as pl
from jax.experimental.pallas import tpu as pltpu
from jax.sharding import PartitionSpec as P

MESH = pl.DeviceIdType.MESH
DH = 128
HALF = DH // 2
UNROLL = 8
EPS = 1e-06
F32 = jnp.float32
BF16 = jnp.bfloat16

PLAN = (
    ("total_a", (0, 1, 2, 3)),
    ("before_a", (2, 3, 4, 5)),
    ("chip_a", (0, 1, 2, 3)),
    ("total_b", (7, 9, 10, 11)),
    ("carry_a", (2, 3, 4, 6)),
    ("carry_b", (10, 11, 12, 13)),
    ("inner", (3, 4, 5, 7)),
    ("forward", (4, 6, 7, 8)),
    ("chip_b", (7, 9, 10, 11)),
    ("query", (5, 6, 7, 12)),
    ("before_b", (9, 10, 11, 12)),
    ("final", (11, 13, 14, 15)),
)


def dot_nn(a, b):
    return lax.dot_general(a, b, (((1,), (0,)), ((), ())), preferred_element_type=F32)


def dot_nt(a, b):
    return lax.dot_general(a, b, (((1,), (1,)), ((), ())), preferred_element_type=F32)


def dot_tn(a, b):
    return lax.dot_general(a, b, (((0,), (0,)), ((), ())), preferred_element_type=F32)


def feature_map(x):
    xf = x.astype(F32)
    return jnp.where(xf > 0, xf + 1.0, jnp.exp(jnp.minimum(xf, 0.0)))


def feature_slope(x):
    xf = x.astype(F32)
    return jnp.where(xf > 0, 1.0, jnp.exp(jnp.minimum(xf, 0.0)))


def kernel(
    groups, nz, npos,
    q_hbm, k_hbm, v_hbm, g_hbm,
    out_ref, gq_ref, gk_ref, gv_ref,
    q_in, k_in, v_in, g_in, q_feat, k_feat, gy_buf, mix_buf, pk_buf, pv_buf,
    load_sem, scan_a, scan_b,
):
    seq = lax.axis_index("seq")
    z = lax.axis_index("head")
    core = lax.rem(seq, 2)
    pos = lax.div(seq, 2)
    sibling = (seq + 1 - 2 * core, z)

    def z_peer(d):
        return lax.rem(z + d, nz)

    def loads(k, *chosen):
        cols = pl.ds(pl.multiple_of(k * (nz * DH), nz * DH), nz * DH)
        pairs = ((k_hbm, k_in), (v_hbm, v_in), (q_hbm, q_in), (g_hbm, g_in))
        return [
            pltpu.make_async_copy(src.at[:, cols], dst.at[:, cols], load_sem.at[i, k])
            for i, (src, dst) in enumerate(pairs)
            if i in chosen
        ]

    def start_loads(*chosen):
        def one(k, _):
            for copy in loads(k, *chosen):
                copy.start()
            return 0

        lax.fori_loop(0, groups, one, 0)

    start_loads(0, 1)
    start_loads(2, 3)

    barrier = pltpu.get_barrier_semaphore()
    pl.semaphore_signal(barrier, inc=1, device_id=sibling, device_id_type=MESH)

    def greet_z(d, _):
        pl.semaphore_signal(barrier, inc=1, device_id=(seq, z_peer(d)), device_id_type=MESH)
        return 0

    def greet_pos(d, _):
        other = lax.rem(pos + d, npos) * 2 + core
        pl.semaphore_signal(barrier, inc=1, device_id=(other, z), device_id_type=MESH)
        return 0

    lax.fori_loop(1, nz, greet_z, 0)
    lax.fori_loop(1, npos, greet_pos, 0)

    row = lax.broadcasted_iota(jnp.int32, (DH, DH), 0)
    col = lax.broadcasted_iota(jnp.int32, (DH, DH), 1)
    lower = row >= col
    upper = col >= row

    unroll = min(UNROLL, nz)

    def each_head(k, body):
        def step(i, _):
            for u in range(unroll):
                o = i * unroll + u
                body(o, pl.ds(pl.multiple_of((k * nz + o) * DH, DH), DH))
            return 0

        lax.fori_loop(0, nz // unroll, step, 0)

    def spread(bufs, name_src, name_dst, name_send, name_recv, k):
        src, dst = bufs[name_src], bufs[name_dst]

        def one(d, _):
            j = nz - d
            side = lax.rem(j, 2)
            peer = z_peer(side * lax.div(j + 1, 2) + (1 - side) * (nz - lax.div(j, 2)))
            pltpu.make_async_remote_copy(
                src_ref=src.at[k, peer], dst_ref=dst.at[k, z],
                send_sem=bufs[name_send].at[k], recv_sem=bufs[name_recv].at[k],
                device_id=(seq, peer), device_id_type=MESH,
            ).start()
            return 0

        lax.fori_loop(1, nz, one, 0)
        dst[k, z] = src[k, z]

    def spread_desc(bufs, name_src, name_dst, name_send, name_recv, k):
        return pltpu.make_async_remote_copy(
            src_ref=bufs[name_src].at[k, pl.ds(0, nz - 1)],
            dst_ref=bufs[name_dst].at[k, pl.ds(0, nz - 1)],
            send_sem=bufs[name_send].at[k], recv_sem=bufs[name_recv].at[k],
            device_id=(seq, z_peer(1)), device_id_type=MESH,
        )

    IN = ("own", "held", "s_in", "r_in")
    BACK = ("ready", "carried", "s_back", "r_back")

    def sib_total(bufs, k):
        return pltpu.make_async_remote_copy(
            src_ref=bufs["total"].at[k, 1 - core], dst_ref=bufs["sib"].at[k],
            send_sem=bufs["s_sib"].at[0, k], recv_sem=bufs["r_sib"].at[0, k],
            device_id=sibling, device_id_type=MESH,
        )

    def sib_before(bufs, k):
        return pltpu.make_async_remote_copy(
            src_ref=bufs["half"].at[k], dst_ref=bufs["before"].at[k, core],
            send_sem=bufs["s_sib"].at[1, k], recv_sem=bufs["r_sib"].at[1, k],
            device_id=sibling, device_id_type=MESH,
        )

    def pos_copy(bufs, k, slot, other):
        return pltpu.make_async_remote_copy(
            src_ref=bufs["chip"].at[k], dst_ref=bufs["chips"].at[k, slot],
            send_sem=bufs["s_pos"].at[k, other], recv_sem=bufs["r_pos"].at[k, slot],
            device_id=(other * 2 + core, z), device_id_type=MESH,
        )

    def targets(forward):
        return (pos + 1, npos) if forward else (0, pos)

    def sources(forward):
        return (0, pos) if forward else (pos + 1, npos)

    def total_stage(bufs, forward, k):
        spread_desc(bufs, *IN, k).wait_recv()
        held = bufs["held"]
        total = held[k, 0].astype(F32)
        for i in range(1, nz):
            total = total + held[k, i].astype(F32)
        bufs["total"][k, 0] = total[:HALF]
        bufs["total"][k, 1] = total[HALF:]
        sib_total(bufs, k).start()

    def chip_stage(bufs, forward, k):
        sib_total(bufs, k).wait_recv()
        bufs["chip"][k] = (bufs["total"][k, core] + bufs["sib"][k]).astype(BF16)

        def one(other, _):
            pos_copy(bufs, k, pos, other).start()
            return 0

        lax.fori_loop(*targets(forward), one, 0)

    def before_stage(bufs, forward, k):
        def one(src, acc):
            pos_copy(bufs, k, src, src).wait_recv()
            return acc + bufs["chips"][k, src].astype(F32)

        earlier = lax.fori_loop(*sources(forward), one, jnp.zeros((HALF, DH), F32))
        first = core == (0 if forward else 1)
        bufs["before"][k, core] = jnp.where(first, earlier, earlier + bufs["sib"][k])
        bufs["half"][k] = jnp.where(first, earlier + bufs["total"][k, core], earlier)
        sib_before(bufs, k).start()

    def carry_stage(bufs, forward, k):
        sib_before(bufs, k).wait_recv()
        before = bufs["before"]
        run = jnp.concatenate([before[k, 0], before[k, 1]], axis=0)
        order = range(nz) if forward else range(nz - 1, -1, -1)
        for i in order:
            bufs["ready"][k, i] = run.astype(BF16)
            run = run + bufs["held"][k, i].astype(F32)
        spread(bufs, *BACK, k)

    def drain(bufs, forward):
        def one(k, _):
            spread_desc(bufs, *IN, k).wait_send()
            spread_desc(bufs, *BACK, k).wait_send()
            sib_total(bufs, k).wait_send()
            sib_before(bufs, k).wait_send()

            def sent(other, _):
                pos_copy(bufs, k, pos, other).wait_send()
                return 0

            lax.fori_loop(*targets(forward), sent, 0)
            return 0

        lax.fori_loop(0, groups, one, 0)

    def keys_compute(k):
        for copy in loads(k, 0, 1):
            copy.wait()

        def body(o, ds):
            kf = feature_map(k_in[:, ds]).astype(BF16)
            k_feat[:, ds] = kf
            scan_a["own"][k, o] = dot_tn(kf, v_in[:, ds]).astype(BF16)

        each_head(k, body)

    def inner_stage(k):
        loads(k, 2)[0].wait()

        def body(o, ds):
            qf = feature_map(q_in[:, ds]).astype(BF16)
            q_feat[:, ds] = qf
            scores = jnp.where(lower, dot_nt(qf, k_feat[:, ds]), 0.0).astype(BF16)
            mix_buf[:, ds] = dot_nn(scores, v_in[:, ds])

        each_head(k, body)

    def forward_stage(k):
        loads(k, 3)[0].wait()
        spread_desc(scan_a, *BACK, k).wait_recv()

        def body(o, ds):
            qf = q_feat[:, ds]
            mixed = mix_buf[:, ds] + dot_nn(qf, scan_a["carried"][k, o])
            inv = lax.rsqrt(jnp.mean(mixed * mixed, -1, keepdims=True) + EPS)
            normed = mixed * inv
            out_ref[:, ds] = normed.astype(BF16)
            grad = g_in[:, ds].astype(F32)
            gy = inv * (grad - normed * jnp.mean(grad * normed, -1, keepdims=True))
            gy = gy.astype(BF16)
            gy_buf[:, ds] = gy
            scan_b["own"][k, o] = dot_tn(qf, gy).astype(BF16)

        each_head(k, body)
        spread(scan_b, *IN, k)

    def query_stage(k):
        def body(o, ds):
            qf, kf, gy, v = q_feat[:, ds], k_feat[:, ds], gy_buf[:, ds], v_in[:, ds]
            m = jnp.where(lower, dot_nt(gy, v), 0.0).astype(BF16)
            dq = dot_nt(gy, scan_a["carried"][k, o]) + dot_nn(m, kf)
            gq_ref[:, ds] = (dq * feature_slope(q_in[:, ds])).astype(BF16)
            mt = jnp.where(upper, dot_nt(v, gy), 0.0).astype(BF16)
            pk_buf[:, ds] = dot_nn(mt, qf)
            at = jnp.where(upper, dot_nt(kf, qf), 0.0).astype(BF16)
            pv_buf[:, ds] = dot_nn(at, gy)

        each_head(k, body)

    def final_stage(k):
        spread_desc(scan_b, *BACK, k).wait_recv()

        def body(o, ds):
            u = scan_b["carried"][k, o]
            dk = dot_nt(v_in[:, ds], u) + pk_buf[:, ds]
            gk_ref[:, ds] = (dk * feature_slope(k_in[:, ds])).astype(BF16)
            gv_ref[:, ds] = (dot_nn(k_feat[:, ds], u) + pv_buf[:, ds]).astype(BF16)

        each_head(k, body)

    keys_compute(0)
    pl.semaphore_wait(barrier, nz + npos - 1)
    spread(scan_a, *IN, 0)

    def start_group(k, _):
        keys_compute(k)
        spread(scan_a, *IN, k)
        return 0

    lax.fori_loop(1, groups, start_group, 0)

    stages = {
        "total_a": functools.partial(total_stage, scan_a, True),
        "chip_a": functools.partial(chip_stage, scan_a, True),
        "before_a": functools.partial(before_stage, scan_a, True),
        "carry_a": functools.partial(carry_stage, scan_a, True),
        "total_b": functools.partial(total_stage, scan_b, False),
        "chip_b": functools.partial(chip_stage, scan_b, False),
        "before_b": functools.partial(before_stage, scan_b, False),
        "carry_b": functools.partial(carry_stage, scan_b, False),
        "inner": inner_stage,
        "forward": forward_stage,
        "query": query_stage,
        "final": final_stage,
    }

    def tick(t, _):
        for name, at in PLAN:
            here = functools.reduce(jnp.logical_or, [t == a for a in at])

            @pl.when(here)
            def _():
                with jax.named_scope(name):
                    stages[name](sum((t >= a).astype(jnp.int32) for a in at[1:]))

        return 0

    lax.fori_loop(0, 1 + max(max(at) for _, at in PLAN), tick, 0)
    drain(scan_a, True)
    drain(scan_b, False)


def scan_buffers(groups, nz, npos):
    dma = pltpu.SemaphoreType.DMA
    states = pltpu.VMEM((groups, nz, DH, DH), BF16)
    halves = pltpu.VMEM((groups, HALF, DH), F32)
    wholes = pltpu.VMEM((groups, 2, HALF, DH), F32)
    return {
        "own": states, "held": states, "ready": states, "carried": states,
        "total": wholes, "before": wholes, "sib": halves, "half": halves,
        "chip": pltpu.VMEM((groups, HALF, DH), BF16),
        "chips": pltpu.VMEM((groups, npos, HALF, DH), BF16),
        "s_in": dma((groups,)), "r_in": dma((groups,)),
        "s_back": dma((groups,)), "r_back": dma((groups,)),
        "s_sib": dma((2, groups)), "r_sib": dma((2, groups)),
        "s_pos": dma((groups, npos)), "r_pos": dma((groups, npos)),
    }


def solution(mesh):
    nz = mesh.shape["head"]
    npos = mesh.shape["seq"] // 2
    placed = P(("seq", "head"), None)

    def local(queries, keys, values, grad_out):
        rows, width = queries.shape
        groups = width // DH // nz
        half = pltpu.VMEM((rows, width), BF16)
        full = pltpu.VMEM((rows, width), F32)
        return pl.pallas_call(
            functools.partial(kernel, groups, nz, npos),
            out_shape=[jax.ShapeDtypeStruct((rows, width), BF16)] * 4,
            in_specs=[pl.BlockSpec(memory_space=pltpu.HBM)] * 4,
            out_specs=[pl.BlockSpec(memory_space=pltpu.VMEM)] * 4,
            scratch_shapes=[half] * 7 + [full] * 3 + [
                pltpu.SemaphoreType.DMA((4, groups)),
                scan_buffers(groups, nz, npos),
                scan_buffers(groups, nz, npos),
            ],
            compiler_params=pltpu.CompilerParams(
                collective_id=0, has_side_effects=True, vmem_limit_bytes=49 * 2**20
            ),
        )(queries, keys, values, grad_out)

    return jax.shard_map(
        local, mesh=mesh, in_specs=(placed,) * 4, out_specs=(placed,) * 4, check_vma=False
    )
```
